256 devices in a mesh: dp: 32 (over z, y_hi, core), grp: 8 (over y_lo, x).
Axes of the slice: x: 4, y: 4 (y_hi: 2, y_lo: 2; y = y_hi * 2 + y_lo), z: 8, core: 2. Of those that a mesh axis runs over, the one named last changes fastest.
Arguments:
- activations: bfloat16 [8192, 1280], P('dp'), may hold values from -12 to 12
- out_grads: bfloat16 [8192, 5120], P('dp'), may hold values from -12 to 12
- basis_a: bfloat16 [1280, 1280], P('grp'), may hold values from -2 to 2
- basis_g: bfloat16 [5120, 5120], P('grp'), may hold values from -2 to 2
Outputs:
- preconditioned: bfloat16 [1280, 5120], P('grp', 'dp')
The draws below stay inside these ranges and needn't reach their ends.
All inputs are finite; a program needn't handle non-finite values.
Results may differ from the reference program's by a relative error of at most 0.027.
Values may be sent and summed in bfloat16 or wider, within the bound.
A program may use at most 64 MiB of HBM per device.

```python
import math
import jax
import jax.numpy as jnp
from jax import lax

D = 1280
F = 5120
TOK_DEV = 256
TOKENS = 8192
N_DP = 32


def scaled_rows(key, rows, width, lowest, highest):
    key_scale = jax.random.fold_in(key, 21)
    key_value = jax.random.fold_in(key, 22)
    scales = jnp.exp(jax.random.uniform(key_scale, (width,), jnp.float32, jnp.log(lowest), jnp.log(highest)))
    values = jax.random.normal(key_value, (rows, width), jnp.float32)
    return jnp.clip(values, -6.0, 6.0) * scales[None, :]


def near_identity(key, width, spread):
    values = jnp.clip(jax.random.normal(key, (width, width), jnp.float32), -6.0, 6.0)
    return jnp.eye(width, dtype=jnp.float32) + spread * values / jnp.sqrt(width * 1.0)


def draw_activations(key, part):
    key = jax.random.fold_in(key, 1)
    values = scaled_rows(key, TOKENS, D, 0.5, 2.0)
    return values.astype(jnp.bfloat16)


def draw_out_grads(key, part):
    key = jax.random.fold_in(key, 2)
    values = scaled_rows(key, TOKENS, F, 0.5, 2.0)
    return values.astype(jnp.bfloat16)


def draw_basis_a(key, part):
    key = jax.random.fold_in(key, 3)
    values = near_identity(key, D, 0.25)
    return values.astype(jnp.bfloat16)


def draw_basis_g(key, part):
    key = jax.random.fold_in(key, 4)
    values = near_identity(key, F, 0.25)
    return values.astype(jnp.bfloat16)


def setup_inputs(seed: int = 0) -> dict:
    arg_keys = jax.random.split(jax.random.key(seed), 5)
    activations = draw_activations(jax.random.fold_in(arg_keys[4], 71), 0)
    out_grads = draw_out_grads(jax.random.fold_in(arg_keys[4], 71), 0)
    basis_a = draw_basis_a(jax.random.fold_in(arg_keys[4], 71), 0)
    basis_g = draw_basis_g(jax.random.fold_in(arg_keys[4], 71), 0)
    return dict(activations=activations, out_grads=out_grads, basis_a=basis_a, basis_g=basis_g)


epsilon = 1e-06
damping = 0.1

def factor(rows):
    width = rows.shape[1]
    blocks = rows.reshape(N_DP, TOK_DEV, width)

    def add_block(total, block):
        part = jnp.dot(block.T, block, preferred_element_type=jnp.float32).astype(jnp.bfloat16)
        part = lax.optimization_barrier(part)
        return (total + part.astype(jnp.float32), None)
    total, _ = lax.scan(add_block, jnp.zeros((width, width), jnp.float32), blocks)
    return total / (TOK_DEV * N_DP)

def refresh(matrix, old_basis):
    projected = jnp.dot(matrix, old_basis.astype(jnp.float32), precision=lax.Precision.HIGHEST)
    scales = jnp.sqrt(lax.optimization_barrier(jnp.sum(projected * projected, axis=0)) + epsilon)
    return ((projected / scales[None, :]).astype(jnp.bfloat16), scales)

def reference(activations, out_grads, basis_a, basis_g):
    fresh_a, scale_a = refresh(factor(activations), basis_a)
    fresh_g, scale_g = refresh(factor(out_grads), basis_g)
    summed = jnp.dot(activations.T, out_grads, preferred_element_type=jnp.float32)
    grad = (summed / math.sqrt(TOK_DEV * N_DP)).astype(jnp.bfloat16)
    rotated = jnp.dot(fresh_a.T, grad, preferred_element_type=jnp.float32).astype(jnp.bfloat16)
    eigen = jnp.dot(rotated, fresh_g, preferred_element_type=jnp.float32)
    scaled = (eigen / (scale_a[:, None] * scale_g[None, :] + damping)).astype(jnp.bfloat16)
    back = jnp.dot(fresh_a, scaled, preferred_element_type=jnp.float32).astype(jnp.bfloat16)
    return jnp.dot(back, fresh_g.T, preferred_element_type=jnp.float32).astype(jnp.bfloat16)
```

```python
import functools
import math

import jax
import jax.numpy as jnp
from jax import lax
from jax.experimental import pallas as pl
from jax.experimental.pallas import tpu as pltpu
from jax.sharding import PartitionSpec as P

epsilon = 1e-06
damping = 0.1

BF16 = jnp.bfloat16
F32 = jnp.float32
NZ = 8
NG = 8
SPLIT = ((0, 48), (48, 32))


def place():
    dp = lax.axis_index("dp")
    grp = lax.axis_index("grp")
    return grp, dp // 4, (dp // 2) % 2, dp % 2


def member(z, yh, c):
    return z * 4 + yh * 2 + c


class Wires:
    def __init__(self, send, recv):
        self.send, self.recv, self.used, self.open = send, recv, 0, []

    def copy(self, src, dst, dp, grp):
        n = self.used
        self.used += 1
        made = pltpu.make_async_remote_copy(
            src_ref=src,
            dst_ref=dst,
            send_sem=self.send.at[n],
            recv_sem=self.recv.at[n],
            device_id=(dp, grp),
            device_id_type=pl.DeviceIdType.MESH,
        )
        self.open.append(made)
        return made

    def drain(self):
        for made in self.open:
            made.wait_send()


def greet(peers):
    barrier = pltpu.get_barrier_semaphore()
    for dp, grp in peers:
        pl.semaphore_signal(barrier, inc=1, device_id=(dp, grp), device_id_type=pl.DeviceIdType.MESH)
    pl.semaphore_wait(barrier, len(peers))


def peers_of(grp, z, yh, c):
    dp = member(z, yh, c)
    found = [(member(z, yh, 1 - c), grp), (member(z, 1 - yh, c), grp)]
    found += [(member((z + r) % NZ, yh, c), grp) for r in range(1, NZ)]
    found += [(dp, (grp + r) % NG) for r in range(1, NG)]
    return found


def add_rows(rows, step, store, loads):
    def body(n, carry):
        at = pl.ds(pl.multiple_of(n * step, step), step)
        total = loads[0](at).astype(F32)
        for load in loads[1:]:
            total = total + load(at).astype(F32)
        store(at, total)
        return carry

    lax.fori_loop(0, rows // step, body, 0)


FW_COPIES = 16 + 14 + 1
A_COPIES = 1 + 7 + 1 + 7 + 1 + 7 + 7 + 7 + 7


def factor_kernel(
    part, part_a, b_own, f_out, w_out, pa_out,
    pair, sent, got, final, other,
    a_pair, a_sent, a_got, a_mine, a_other, a_full, b_full, send, recv,
):
    grp, z, yh, c = place()
    me = member(z, yh, c)
    twin = member(z, yh, 1 - c)
    far = member(z, 1 - yh, c)
    greet(peers_of(grp, z, yh, c))
    wires = Wires(send, recv)

    a_swap = wires.copy(part_a.at[1 - c], a_pair, twin, grp)
    a_swap.start()
    swaps = {}
    for r, h in ((4, 0), (4, 1), (3, 1), (5, 0), (3, 0), (5, 1), (2, 1), (6, 0), (2, 0), (6, 1),
                 (1, 1), (7, 0), (1, 0), (7, 1), (0, 0), (0, 1)):
        zz = (z + r) % NZ
        swaps[r, h] = wires.copy(part.at[(zz * 2 + h) * 2 + 1 - c], pair.at[r * 2 + h], twin, grp)
        swaps[r, h].start()
    b_in = []
    for r in range(1, NG):
        b_in.append(wires.copy(b_own.at[c], b_full.at[grp, c], me, (grp + r) % NG))
        b_in[-1].start()
    b_full[grp] = b_own[...]

    a_swap.wait_recv()
    a_in = []
    for r in range(1, NZ):
        zz = (z + r) % NZ
        a_sent[r - 1] = (part_a[c, zz].astype(F32) + a_pair[zz].astype(F32)).astype(BF16)
        a_in.append(wires.copy(a_sent.at[r - 1], a_got.at[r - 1], member(zz, yh, c), grp))
        a_in[-1].start()

    ring = {}

    def tile_loads(r, h):
        own = ((z + r) % NZ * 2 + h) * 2 + c
        return [lambda at: part[own, at, :], lambda at: pair[r * 2 + h, at, :]]

    def hop(way, h, d):
        sign = 1 if way == 0 else -1
        r = (sign * d) % NZ
        swaps[r, h].wait_recv()
        loads = tile_loads(r, h)
        if (way, h, d) in ring:
            ring[way, h, d].wait_recv()
            loads.append(lambda at: got[way, h, d, at, :])

        def store(at, total):
            sent[way, h, d - 1, at, :] = total.astype(BF16)

        add_rows(160, 32, store, loads)
        to = member((z + sign) % NZ, yh, c)
        ring[way, h, d - 1] = wires.copy(sent.at[way, h, d - 1], got.at[way, h, d - 1], to, grp)
        ring[way, h, d - 1].start()

    hop(0, 0, 4)
    hop(1, 1, 4)
    hop(0, 1, 3)
    hop(1, 0, 3)
    hop(0, 0, 3)
    hop(1, 1, 3)

    for made in a_in:
        made.wait_recv()
    total = part_a[c, z].astype(F32) + a_pair[z].astype(F32)
    for r in range(1, NZ):
        total = total + a_got[r - 1].astype(F32)
    a_mine[...] = total.astype(BF16)
    a_far = wires.copy(a_mine, a_other, far, grp)
    a_far.start()

    hop(0, 1, 2)
    hop(1, 0, 2)

    a_far.wait_recv()
    a_full[c, z] = ((a_mine[...].astype(F32) + a_other[...].astype(F32)) / 8192.0).astype(BF16)
    a_rows = []
    for r in range(1, NZ):
        to = member((z + r) % NZ, yh, c)
        a_rows.append(wires.copy(a_full.at[c, z], a_full.at[c, z], to, grp))
        a_rows[-1].start()

    hop(0, 0, 2)
    hop(1, 1, 2)

    b_on = []
    for r in range(1, NG):
        b_in[r - 1].wait_recv()
        owner = (grp + NG - r) % NG
        b_on.append(wires.copy(b_full.at[owner, c], b_full.at[owner, c], twin, grp))
        b_on[-1].start()
    for made in a_rows:
        made.wait_recv()
    a_half = wires.copy(a_full.at[c], a_full.at[c], twin, grp)
    a_half.start()

    hop(0, 1, 1)
    hop(1, 0, 1)

    a_half.wait_recv()
    for made in b_on:
        made.wait_recv()
    left = a_full[...].reshape(1280, 160)

    for n in range(5):
        at = pl.ds(n * 256, 256)
        right = b_full[:, :, :, at].reshape(1280, 256)
        product = lax.dot_general(left, right, (((0,), (0,)), ((), ())), preferred_element_type=F32)
        pa_out[grp, :, :, at] = product.astype(BF16).reshape(2, 80, 256)
    p_in = []
    for r in range(1, NG):
        p_in.append(wires.copy(pa_out.at[grp, c], pa_out.at[grp, c], me, (grp + r) % NG))
        p_in[-1].start()

    hop(0, 0, 1)
    hop(1, 1, 1)

    for h in range(2):
        swaps[0, h].wait_recv()
        ring[0, h, 0].wait_recv()
        ring[1, h, 0].wait_recv()
        loads = tile_loads(0, h)
        loads.append(lambda at, h=h: got[0, h, 0, at, :])
        loads.append(lambda at, h=h: got[1, h, 0, at, :])

        def store(at, total, h=h):
            final[h, at, :] = total.astype(BF16)

        add_rows(160, 32, store, loads)
    across = wires.copy(final.at[1 - yh], other, far, grp)
    across.start()

    p_on = []
    for r in range(1, NG):
        p_in[r - 1].wait_recv()
        owner = (grp + NG - r) % NG
        p_on.append(wires.copy(pa_out.at[owner, c], pa_out.at[owner, c], twin, grp))
        p_on[-1].start()

    across.wait_recv()

    def finish(at, total):
        f_out[at, :] = (total[:, :640] / 8192.0).astype(BF16)
        w_out[at, :] = total[:, 640:].astype(BF16)

    add_rows(160, 32, finish, [lambda at: final[yh, at, :], lambda at: other[at, :]])
    for made in p_on:
        made.wait_recv()
    wires.drain()


def factors(part, part_a, b_own):
    vmem = pl.BlockSpec(memory_space=pltpu.VMEM)
    copies = FW_COPIES + A_COPIES
    return pl.pallas_call(
        factor_kernel,
        name="factors",
        out_shape=(
            jax.ShapeDtypeStruct((160, 640), BF16),
            jax.ShapeDtypeStruct((160, 160), BF16),
            jax.ShapeDtypeStruct((8, 2, 80, 1280), BF16),
        ),
        in_specs=[vmem] * 3,
        out_specs=(vmem, vmem, vmem),
        scratch_shapes=[
            pltpu.VMEM((16, 160, 800), BF16),
            pltpu.VMEM((2, 2, 4, 160, 800), BF16),
            pltpu.VMEM((2, 2, 4, 160, 800), BF16),
            pltpu.VMEM((2, 160, 800), BF16),
            pltpu.VMEM((160, 800), BF16),
            pltpu.VMEM((8, 80, 160), BF16),
            pltpu.VMEM((7, 80, 160), BF16),
            pltpu.VMEM((7, 80, 160), BF16),
            pltpu.VMEM((80, 160), BF16),
            pltpu.VMEM((80, 160), BF16),
            pltpu.VMEM((2, 8, 80, 160), BF16),
            pltpu.VMEM((8, 2, 80, 1280), BF16),
            pltpu.SemaphoreType.DMA((copies,)),
            pltpu.SemaphoreType.DMA((copies,)),
        ],
        compiler_params=pltpu.CompilerParams(
            collective_id=0, has_side_effects=True, vmem_limit_bytes=56 * 2**20
        ),
        cost_estimate=pl.CostEstimate(flops=10**9, bytes_accessed=10**7, transcendentals=0),
    )(part, part_a, b_own)


def project_kernel(f, w, b, p_out, w_full, sent, got, send, recv):
    grp, z, yh, c = place()
    me = member(z, yh, c)
    greet([(me, (grp + r) % NG) for r in range(1, NG)])
    wires = Wires(send, recv)
    w_full[grp] = w[...]
    w_in = []
    p_in = []

    def product(owner):
        at = pl.ds(pl.multiple_of(owner * 640, 128), 640)
        return jnp.dot(f[...], b[:, at], preferred_element_type=F32)

    for r in range(1, NG):
        to = (grp + r) % NG
        sent[r - 1] = product(to).astype(BF16)
        p_in.append(wires.copy(sent.at[r - 1], got.at[r - 1], me, to))
        p_in[-1].start()
    for r in range(1, NG):
        to = (grp + r) % NG
        w_in.append(wires.copy(w_full.at[grp], w_full.at[grp], me, to))
        w_in[-1].start()
    sent[7] = product(grp).astype(BF16)
    for made in p_in:
        made.wait_recv()

    def store(at, total):
        p_out[at, :] = total.astype(BF16)

    add_rows(160, 32, store, [lambda at: sent[7, at, :]] + [lambda at, r=r: got[r, at, :] for r in range(7)])
    for made in w_in:
        made.wait_recv()
    wires.drain()


def project(f, w, b):
    vmem = pl.BlockSpec(memory_space=pltpu.VMEM)
    return pl.pallas_call(
        project_kernel,
        name="project",
        out_shape=(
            jax.ShapeDtypeStruct((160, 640), BF16),
            jax.ShapeDtypeStruct((8, 160, 160), BF16),
        ),
        in_specs=[vmem] * 3,
        out_specs=(vmem, vmem),
        scratch_shapes=[
            pltpu.VMEM((8, 160, 640), BF16),
            pltpu.VMEM((7, 160, 640), BF16),
            pltpu.SemaphoreType.DMA((14,)),
            pltpu.SemaphoreType.DMA((14,)),
        ],
        compiler_params=pltpu.CompilerParams(
            collective_id=1, has_side_effects=True, vmem_limit_bytes=56 * 2**20
        ),
        cost_estimate=pl.CostEstimate(flops=10**9, bytes_accessed=10**7, transcendentals=0),
    )(f, w, b)


PRECONDITION_COPIES = 2 + 7 + 1 + 14 + 1 + 14 + 16 + 7


def precondition_kernel(
    w_full, pa, p, scale_a, out,
    rot, rot_twin, p_twin, eig, norm, norm_got, norm_mine, norm_other,
    sent, got, mine, other, scaled, o_sent, o_got, send, recv,
):
    grp, z, yh, c = place()
    me = member(z, yh, c)
    twin = member(z, yh, 1 - c)
    far = member(z, 1 - yh, c)
    greet(peers_of(grp, z, yh, c))
    wires = Wires(send, recv)

    p_swap = wires.copy(p, p_twin, twin, grp)
    p_swap.start()
    for h in range(2):
        at = pl.ds(h * 640, 640)
        total = jnp.zeros((160, 640), F32)
        for n in range(NG):
            total = total + jnp.dot(w_full[n], pa[n * 160 : n * 160 + 160, at], preferred_element_type=F32)
        rot[h] = total.astype(BF16)
    r_swap = wires.copy(rot.at[1 - c], rot_twin, twin, grp)
    r_swap.start()

    p_swap.wait_recv()
    wide = p[...].astype(F32)
    wide_twin = p_twin[...].astype(F32)
    squares = jnp.sum(wide * wide, axis=0, keepdims=True) + jnp.sum(wide_twin * wide_twin, axis=0, keepdims=True)
    norm[...] = jnp.broadcast_to(squares, (8, 640))
    n_in = []
    for r in range(1, NZ):
        n_in.append(wires.copy(norm, norm_got.at[r - 1], member((z + r) % NZ, yh, c), grp))
        n_in[-1].start()

    r_swap.wait_recv()
    across = (((0,), (0,)), ((), ()))
    eigen = lax.dot_general(rot[c], p[...], across, preferred_element_type=F32)
    eigen = eigen + lax.dot_general(rot_twin[...], p_twin[...], across, preferred_element_type=F32)
    eig[...] = eigen.reshape(8, 80, 640)

    ring = {}

    def hop(way, h, d):
        sign = 1 if way == 0 else -1
        start, rows = SPLIT[h]
        at = pl.ds(start, rows)
        into = pl.ds(0, rows)
        zz = (z + sign * d + NZ) % NZ
        total = eig[zz, at, :]
        if (way, h, d) in ring:
            ring[way, h, d].wait_recv()
            total = total + got[way, h, d, into, :].astype(F32)
        sent[way, h, d - 1, into, :] = total.astype(BF16)
        to = member((z + sign + NZ) % NZ, yh, c)
        ring[way, h, d - 1] = wires.copy(
            sent.at[way, h, d - 1, into, :], got.at[way, h, d - 1, into, :], to, grp
        )
        ring[way, h, d - 1].start()

    hop(0, 0, 4)
    hop(1, 1, 4)
    hop(0, 1, 3)
    hop(1, 0, 3)
    for d in (3, 2, 1):
        hop(0, 0, d)
        hop(1, 1, d)
        if d > 1:
            hop(0, 1, d - 1)
            hop(1, 0, d - 1)
        if d == 3:
            for made in n_in:
                made.wait_recv()
            total = norm[...]
            for r in range(1, NZ):
                total = total + norm_got[r - 1]
            norm_mine[...] = total
            n_far = wires.copy(norm_mine, norm_other, far, grp)
            n_far.start()

    for h in range(2):
        start, rows = SPLIT[h]
        at = pl.ds(start, rows)
        into = pl.ds(0, rows)
        ring[0, h, 0].wait_recv()
        ring[1, h, 0].wait_recv()
        total = eig[z, at, :] + got[0, h, 0, into, :].astype(F32) + got[1, h, 0, into, :].astype(F32)
        mine[at, :] = total.astype(BF16)
    e_far = wires.copy(mine, other, far, grp)
    e_far.start()

    n_far.wait_recv()
    scale_g = jnp.sqrt(norm_mine[...] + norm_other[...] + epsilon)[0:1, :]
    scale = scale_a[...][:, 0:1] * scale_g
    e_far.wait_recv()
    eigen = (mine[...].astype(F32) + other[...].astype(F32)) * (1.0 / math.sqrt(8192.0))
    scaled[c, z] = (eigen / scale / (scale + damping) / scale).astype(BF16)

    moves = {}
    to_twin = []

    def pass_on(way, h, d):
        sign = 1 if way == 0 else -1
        at = pl.ds(*SPLIT[h])
        source = (z - sign * d + NZ) % NZ
        view = scaled.at[c, source, at, :]
        if d > 0:
            moves[way, h, d].wait_recv()
        if d < (4 if way == h else 3):
            to = member((z + sign + NZ) % NZ, yh, c)
            moves[way, h, d + 1] = wires.copy(view, view, to, grp)
            moves[way, h, d + 1].start()
        if d > 0 or way == 0:
            to_twin.append(wires.copy(view, view, twin, grp))
            to_twin[-1].start()

    for d in range(5):
        for way, h in ((0, 0), (1, 1), (0, 1), (1, 0)):
            if d <= (4 if way == h else 3):
                pass_on(way, h, d)
    for made in to_twin:
        made.wait_recv()

    rotated = lax.dot_general(
        scaled[...].reshape(1280, 640), p[...], (((1,), (1,)), ((), ())), preferred_element_type=F32
    ).astype(BF16)
    o_in = []
    for r in range(1, NG + 1):
        to = (grp + r) % NG
        rows = pl.ds(pl.multiple_of(to * 160, 32), 160)
        o_sent[r - 1] = jnp.dot(pa[rows, :], rotated, preferred_element_type=F32).astype(BF16)
        if r < NG:
            o_in.append(wires.copy(o_sent.at[r - 1], o_got.at[r - 1], me, to))
            o_in[-1].start()
    total = o_sent[7].astype(F32)
    for r in range(1, NG):
        o_in[r - 1].wait_recv()
        total = total + o_got[r - 1].astype(F32)
    out[...] = total.astype(BF16)
    wires.drain()


def precondition(w_full, pa, p, scale_a):
    vmem = pl.BlockSpec(memory_space=pltpu.VMEM)
    return pl.pallas_call(
        precondition_kernel,
        name="precondition",
        out_shape=jax.ShapeDtypeStruct((160, 160), BF16),
        in_specs=[vmem] * 4,
        out_specs=vmem,
        scratch_shapes=[
            pltpu.VMEM((2, 160, 640), BF16),
            pltpu.VMEM((160, 640), BF16),
            pltpu.VMEM((160, 640), BF16),
            pltpu.VMEM((8, 80, 640), F32),
            pltpu.VMEM((8, 640), F32),
            pltpu.VMEM((7, 8, 640), F32),
            pltpu.VMEM((8, 640), F32),
            pltpu.VMEM((8, 640), F32),
            pltpu.VMEM((2, 2, 4, 48, 640), BF16),
            pltpu.VMEM((2, 2, 4, 48, 640), BF16),
            pltpu.VMEM((80, 640), BF16),
            pltpu.VMEM((80, 640), BF16),
            pltpu.VMEM((2, 8, 80, 640), BF16),
            pltpu.VMEM((8, 160, 160), BF16),
            pltpu.VMEM((7, 160, 160), BF16),
            pltpu.SemaphoreType.DMA((PRECONDITION_COPIES,)),
            pltpu.SemaphoreType.DMA((PRECONDITION_COPIES,)),
        ],
        compiler_params=pltpu.CompilerParams(
            collective_id=2, has_side_effects=True, vmem_limit_bytes=56 * 2**20
        ),
        cost_estimate=pl.CostEstimate(flops=10**9, bytes_accessed=10**7, transcendentals=0),
    )(w_full, pa, p, scale_a)


def stages(activations, out_grads, basis_a, basis_g):
    grp, z, yh, c = place()
    own_a = lax.dynamic_slice_in_dim(activations, grp * 160, 160, 1)
    own_g = lax.dynamic_slice_in_dim(out_grads, grp * 640, 640, 1)
    both = jnp.concatenate([own_g, own_a], axis=1)
    part = jnp.einsum("tf,te->fe", out_grads, both, preferred_element_type=F32).astype(BF16)
    part_a = jnp.einsum("td,te->de", activations, own_a, preferred_element_type=F32).astype(BF16)
    f, w, pa = factors(part.reshape(32, 160, 800), part_a.reshape(2, 8, 80, 160), basis_a.reshape(2, 80, 1280))
    pa = pa.reshape(1280, 1280)
    p, w_full = project(f, w, basis_g)
    wide = pa.astype(F32)
    scale_a = jnp.sqrt(jnp.sum(wide * wide, axis=0) + epsilon).reshape(16, 80)
    scale_a = lax.dynamic_slice_in_dim(scale_a, c * 8 + z, 1, 0).reshape(80, 1)
    scale_a = jnp.broadcast_to(scale_a, (80, 128))
    out = precondition(w_full, pa, p, scale_a)
    return f, w, pa, p, w_full, scale_a, out


def per_device(*args):
    return stages(*args)[-1]


def solution(mesh):
    in_specs = (P("dp", None), P("dp", None), P("grp", None), P("grp", None))
    out_specs = P("grp", "dp")
    return jax.shard_map(per_device, mesh=mesh, in_specs=in_specs, out_specs=out_specs, check_vma=False)
```

```python
import math
import types

import jax
import jax.numpy as jnp
from jax import lax
from jax.experimental import pallas as pl
from jax.experimental.pallas import tpu as pltpu
from jax.sharding import PartitionSpec as P

epsilon = 1e-06
damping = 0.1

BF16 = jnp.bfloat16
F32 = jnp.float32
NZ = 8
NX = 4
NG = 8
COPIES = 256
ROWS = ((0, 48), (48, 32))
COLS = ((0, 384), (384, 256))
STARTS = ((0, 0, 4), (1, 1, 4), (0, 1, 3), (1, 0, 3))


def member(z, yh, c):
    return z * 4 + yh * 2 + c


class Wires:
    def __init__(self, send, recv):
        self.send, self.recv, self.used, self.open = send, recv, 0, []

    def copy(self, src, dst, dp, grp):
        n = self.used
        self.used += 1
        made = pltpu.make_async_remote_copy(
            src_ref=src,
            dst_ref=dst,
            send_sem=self.send.at[n],
            recv_sem=self.recv.at[n],
            device_id=(dp, grp),
            device_id_type=pl.DeviceIdType.MESH,
        )
        made.start()
        self.open.append(made)
        return made

    def drain(self):
        for made in self.open:
            made.wait_send()


def greet(peers):
    barrier = pltpu.get_barrier_semaphore()
    for dp, grp in peers:
        pl.semaphore_signal(barrier, inc=1, device_id=(dp, grp), device_id_type=pl.DeviceIdType.MESH)
    pl.semaphore_wait(barrier, len(peers))


def down_rows(left, right):
    return lax.dot_general(left, right, (((0,), (0,)), ((), ())), preferred_element_type=F32)


class Ring:
    def __init__(self, wires, sent, got, cut, base, send_to):
        self.wires, self.sent, self.got, self.cut, self.base, self.send_to = wires, sent, got, cut, base, send_to
        self.links = {}

    def hop(self, way, h, d):
        total = self.base((d if way == 0 else -d) % NZ, h)
        if (way, h, d) in self.links:
            self.links[way, h, d].wait_recv()
            total = total + self.got[(way, h, d) + self.cut(h)].astype(F32)
        view = (way, h, d - 1) + self.cut(h)
        self.sent[view] = total.astype(BF16)
        dp, grp = self.send_to[way]
        self.links[way, h, d - 1] = self.wires.copy(self.sent.at[view], self.got.at[view], dp, grp)

    def end(self, h):
        total = self.base(0, h)
        for way in range(2):
            self.links[way, h, 0].wait_recv()
            total = total + self.got[(way, h, 0) + self.cut(h)].astype(F32)
        return total


def whole(h):
    return (slice(None), slice(None))


def columns_from_zero(h):
    return (slice(None), pl.ds(0, COLS[h][1]))


SCRATCH = dict(
    tokens_a=((256, 1280), BF16),
    tokens_g=((256, 5120), BF16),
    basis=((640, 5120), BF16),
    own_a=((256, 160), BF16),
    part_a=((2, 8, 80, 160), BF16),
    pair_a=((8, 80, 160), BF16),
    a_sent=((7, 80, 160), BF16),
    a_got=((7, 80, 160), BF16),
    a_mine=((80, 160), BF16),
    a_other=((80, 160), BF16),
    a_full=((2, 8, 80, 160), BF16),
    b_full=((8, 2, 80, 1280), BF16),
    pa=((8, 2, 80, 1280), BF16),
    part_f=((8, 2, 2, 160, 640), BF16),
    part_w=((8, 2, 2, 160, 160), BF16),
    pair_f=((8, 2, 160, 640), BF16),
    pair_w=((8, 2, 160, 160), BF16),
    f_sent=((2, 2, 4, 80, 640), BF16),
    f_got=((2, 2, 4, 80, 640), BF16),
    f_final=((2, 80, 640), BF16),
    f_other=((80, 640), BF16),
    early_sent=((8, 80, 640), BF16),
    early_got=((8, 80, 640), BF16),
    l_sent=((2, 2, 4, 80, 384), BF16),
    l_got=((2, 2, 4, 80, 384), BF16),
    w_sent=((2, 2, 4, 160, 160), BF16),
    w_got=((2, 2, 4, 160, 160), BF16),
    w_final=((2, 160, 160), BF16),
    w_other=((160, 160), BF16),
    w_full=((8, 160, 160), BF16),
    f=((160, 640), BF16),
    p_sent=((8, 160, 640), BF16),
    p_got=((7, 160, 640), BF16),
    p=((160, 640), BF16),
    p_twin=((160, 640), BF16),
    rot=((2, 640, 160), BF16),
    rot_twin=((640, 160), BF16),
    scale_a=((16, 80, 128), F32),
    eig=((8, 80, 640), F32),
    norm=((8, 640), F32),
    norm_got=((7, 8, 640), F32),
    norm_mine=((8, 640), F32),
    norm_other=((8, 640), F32),
    e_sent=((2, 2, 4, 80, 384), BF16),
    e_got=((2, 2, 4, 80, 384), BF16),
    e_mine=((80, 640), BF16),
    e_other=((80, 640), BF16),
    scaled=((2, 8, 80, 640), BF16),
    o_sent=((8, 160, 160), BF16),
    o_got=((7, 160, 160), BF16),
)


def kernel(act, grads, b_own, b_g, out, *scratch):
    s = types.SimpleNamespace(**dict(zip(SCRATCH, scratch)))
    load, send, recv = scratch[len(SCRATCH) :]
    dp = lax.axis_index("dp")
    grp = lax.axis_index("grp")
    z, yh, c = dp // 4, (dp // 2) % 2, dp % 2
    yl, x = grp // NX, grp % NX
    me = dp
    twin = (member(z, yh, 1 - c), grp)
    far = (member(z, 1 - yh, c), grp)
    cross = (1 - yl) * NX + x
    up = (member(z, (yh + yl) % 2, c), cross)
    down = (member(z, (yh + 1 - yl) % 2, c), cross)
    along_z = [(member((z + r) % NZ, yh, c), grp) for r in range(NZ)]
    along_x = [(me, yl * NX + (x + r) % NX) for r in range(NX)]
    ways = (along_z[1], along_z[NZ - 1])
    wires = Wires(send, recv)

    loads = [
        pltpu.make_async_copy(act, s.tokens_a, load.at[0]),
        pltpu.make_async_copy(grads, s.tokens_g, load.at[1]),
        pltpu.make_async_copy(b_g, s.basis, load.at[2]),
    ]
    for made in loads:
        made.start()
    greet(
        [twin, far, (member(z, 1 - yh, c), cross)]
        + along_z[1:]
        + [(me, (grp + r) % NG) for r in range(1, NG)]
    )

    s.b_full[grp] = b_own[...]
    mine_b = s.b_full.at[grp, c]
    b_y = []
    for part, to in enumerate((up, down)):
        view = s.b_full.at[grp, c, pl.ds(*ROWS[part])]
        b_y.append(wires.copy(b_own.at[c, pl.ds(*ROWS[part])], view, *to))
    b_x = [wires.copy(b_own.at[c], mine_b, *along_x[r]) for r in range(1, NX)]
    b_x2 = []
    b_twin = []

    def b_across():
        for made in b_y:
            made.wait_recv()
        view = s.b_full.at[cross, c]
        for r in range(1, NX):
            b_x2.append(wires.copy(view, view, *along_x[r]))
        b_twin.append(wires.copy(view, view, *twin))

    def b_along():
        for row, arrived in ((yl, b_x), (1 - yl, b_x2)):
            for r in range(1, NX):
                arrived[r - 1].wait_recv()
                view = s.b_full.at[row * NX + (x + NX - r) % NX, c]
                b_twin.append(wires.copy(view, view, *twin))

    loads[0].wait()
    first = lax.broadcasted_iota(jnp.int32, (1280, 160), 0)
    second = lax.broadcasted_iota(jnp.int32, (1280, 160), 1)
    chosen = jnp.where(first == second + grp * 160, 1.0, 0.0).astype(BF16)
    s.own_a[...] = jnp.dot(s.tokens_a[...], chosen, preferred_element_type=F32).astype(BF16)
    for half in range(2):
        block = down_rows(s.tokens_a[:, half * 640 : half * 640 + 640], s.own_a[...])
        s.part_a[half] = block.astype(BF16).reshape(8, 80, 160)
    swap_a = wires.copy(s.part_a.at[1 - c], s.pair_a, *twin)

    loads[1].wait()
    own_columns = pl.ds(pl.multiple_of(grp * 640, 128), 640)
    swaps_f, swaps_w, ready_f, ready_w = {}, {}, set(), set()

    def block(r):
        zz = (z + r) % NZ
        left = s.tokens_g[:, pl.ds(pl.multiple_of(zz * 640, 128), 640)]
        for_f = down_rows(left, s.tokens_g[:, own_columns])
        for_w = down_rows(left, s.own_a[...])
        for h in range(2):
            for cc in range(2):
                rows = slice((h * 2 + cc) * 160, (h * 2 + cc) * 160 + 160)
                s.part_f[zz, cc, h] = for_f[rows].astype(BF16)
                s.part_w[zz, cc, h] = for_w[rows].astype(BF16)
        swaps_f[r] = wires.copy(s.part_f.at[zz, 1 - c], s.pair_f.at[r], *twin)
        swaps_w[r] = wires.copy(s.part_w.at[zz, 1 - c], s.pair_w.at[r], *twin)

    def share_f(r, h, rows, cols=slice(None)):
        if r not in ready_f:
            ready_f.add(r)
            swaps_f[r].wait_recv()
        zz = (z + r) % NZ
        return s.part_f[zz, c, h, rows, cols].astype(F32) + s.pair_f[r, h, rows, cols].astype(F32)

    def share_w(r, h):
        if r not in ready_w:
            ready_w.add(r)
            swaps_w[r].wait_recv()
        zz = (z + r) % NZ
        return s.part_w[zz, c, h].astype(F32) + s.pair_w[r, h].astype(F32)

    ring_f = Ring(wires, s.f_sent, s.f_got, whole, lambda r, h: share_f(r, h, slice(0, 80)), ways)
    ring_w = Ring(wires, s.w_sent, s.w_got, whole, share_w, ways)
    early = {}

    def send_early(r):
        s.early_sent[r] = share_f(r, 1 - yh, slice(80, 160)).astype(BF16)
        early[r] = wires.copy(s.early_sent.at[r], s.early_got.at[r], *far)

    early_ready = set()

    def late(r, h):
        if r not in early_ready:
            early_ready.add(r)
            early[r].wait_recv()
        cols = slice(COLS[h][0], COLS[h][0] + COLS[h][1])
        return share_f(r, yh, slice(80, 160), cols) + s.early_got[r, :, cols].astype(F32)

    ring_l = Ring(wires, s.l_sent, s.l_got, columns_from_zero, late, ways)

    block(4)
    block(3)
    swap_a.wait_recv()
    a_in = []
    for r in range(1, NZ):
        zz = (z + r) % NZ
        s.a_sent[r - 1] = (s.part_a[c, zz].astype(F32) + s.pair_a[zz].astype(F32)).astype(BF16)
        a_in.append(wires.copy(s.a_sent.at[r - 1], s.a_got.at[r - 1], *along_z[r]))
    block(5)
    for hop in STARTS:
        ring_f.hop(*hop)
    block(2)
    send_early(4)
    block(6)
    send_early(3)
    block(1)
    send_early(5)
    ring_f.hop(0, 0, 3)
    ring_f.hop(1, 1, 3)
    block(7)
    b_across()
    send_early(2)
    send_early(6)

    for made in a_in:
        made.wait_recv()
    total = s.part_a[c, z].astype(F32) + s.pair_a[z].astype(F32)
    for r in range(1, NZ):
        total = total + s.a_got[r - 1].astype(F32)
    s.a_mine[...] = total.astype(BF16)
    a_far = wires.copy(s.a_mine, s.a_other, *far)

    ring_f.hop(0, 1, 2)
    ring_f.hop(1, 0, 2)
    block(0)
    send_early(1)
    send_early(7)

    a_far.wait_recv()
    s.a_full[c, z] = ((s.a_mine[...].astype(F32) + s.a_other[...].astype(F32)) / 8192.0).astype(BF16)
    a_rows = [wires.copy(s.a_full.at[c, z], s.a_full.at[c, z], *along_z[r]) for r in range(1, NZ)]

    ring_f.hop(0, 0, 2)
    ring_f.hop(1, 1, 2)
    send_early(0)
    ring_f.hop(0, 1, 1)
    ring_f.hop(1, 0, 1)
    ring_f.hop(0, 0, 1)
    ring_f.hop(1, 1, 1)
    for hop in STARTS:
        ring_w.hop(*hop)

    for made in a_rows:
        made.wait_recv()
    a_half = wires.copy(s.a_full.at[c], s.a_full.at[c], *twin)
    b_along()

    for h in range(2):
        s.f_final[h] = ring_f.end(h).astype(BF16)
    f_far = wires.copy(s.f_final.at[1 - yh], s.f_other, *far)

    a_half.wait_recv()
    for made in b_twin:
        made.wait_recv()
    left = s.a_full[...].reshape(1280, 160)
    for n in range(5):
        at = pl.ds(n * 256, 256)
        product = down_rows(left, s.b_full[:, :, :, at].reshape(1280, 256))
        s.pa[grp, :, :, at] = product.astype(BF16).reshape(2, 80, 256)
    pa_y = {}
    pa_twin = []

    def pa_across(r):
        owner = yl * NX + (x + NX - r) % NX
        for part, to in enumerate((up, down)):
            view = s.pa.at[owner, c, pl.ds(*ROWS[part])]
            pa_y[r, part] = wires.copy(view, view, *to)

    pa_x = [wires.copy(s.pa.at[grp, c], s.pa.at[grp, c], *along_x[r]) for r in range(1, NX)]
    pa_across(0)

    ring_w.hop(0, 0, 3)
    ring_w.hop(1, 1, 3)

    loads[2].wait()
    p_in = {}

    def project(n):
        rows = slice(n * 80, n * 80 + 80)
        for r in range(1, NG + 1):
            to = (grp + r) % NG
            at = pl.ds(pl.multiple_of(to * 640, 128), 640)
            chunk = jnp.dot(s.f[rows, :], s.basis[:, at], preferred_element_type=F32)
            s.p_sent[r - 1, rows, :] = chunk.astype(BF16)
            if r < NG:
                for h in range(2):
                    view = (r - 1, pl.ds(n * 80, 80), pl.ds(*COLS[h]))
                    p_in[n, h, r] = wires.copy(s.p_sent.at[view], s.p_got.at[view], me, to)

    def projected(n, h):
        rows, cols = slice(n * 80, n * 80 + 80), slice(COLS[h][0], COLS[h][0] + COLS[h][1])
        total = s.p_sent[NG - 1, rows, cols].astype(F32)
        for r in range(1, NG):
            p_in[n, h, r].wait_recv()
            total = total + s.p_got[r - 1, rows, cols].astype(F32)
        s.p[rows, cols] = total.astype(BF16)

    f_far.wait_recv()
    s.f[0:80, :] = ((s.f_final[yh].astype(F32) + s.f_other[...].astype(F32)) / 8192.0).astype(BF16)
    project(0)

    ring_w.hop(0, 1, 2)
    ring_w.hop(1, 0, 2)
    ring_w.hop(0, 0, 2)
    ring_w.hop(1, 1, 2)
    for r in range(1, NX):
        pa_x[r - 1].wait_recv()
        pa_across(r)
        view = s.pa.at[yl * NX + (x + NX - r) % NX, c]
        pa_twin.append(wires.copy(view, view, *twin))
    ring_w.hop(0, 1, 1)
    ring_w.hop(1, 0, 1)
    ring_w.hop(0, 0, 1)
    ring_w.hop(1, 1, 1)
    for hop in STARTS:
        ring_l.hop(*hop)
    for h in range(2):
        s.w_final[h] = ring_w.end(h).astype(BF16)
    w_far = wires.copy(s.w_final.at[1 - yh], s.w_other, *far)
    ring_l.hop(0, 0, 3)
    ring_l.hop(1, 1, 3)
    ring_l.hop(0, 1, 2)
    ring_l.hop(1, 0, 2)
    w_far.wait_recv()
    s.w_full[grp] = (s.w_final[yh].astype(F32) + s.w_other[...].astype(F32)).astype(BF16)
    w_in = [
        wires.copy(s.w_full.at[grp], s.w_full.at[grp], me, (grp + r) % NG) for r in range(1, NG)
    ]
    for hop in ((0, 0, 2), (1, 1, 2), (0, 1, 1), (1, 0, 1), (0, 0, 1), (1, 1, 1)):
        ring_l.hop(*hop)
    for h in range(2):
        s.f[80:160, COLS[h][0] : COLS[h][0] + COLS[h][1]] = (ring_l.end(h) / 8192.0).astype(BF16)
    project(1)

    for r in range(NX):
        for part in range(2):
            pa_y[r, part].wait_recv()
        view = s.pa.at[(1 - yl) * NX + (x + NX - r) % NX, c]
        pa_twin.append(wires.copy(view, view, *twin))
    projected(0, 0)
    projected(0, 1)
    for made in pa_twin:
        made.wait_recv()
    squares = jnp.zeros((8, 1280), F32)
    for n in range(NG):
        wide = s.pa[n].reshape(160, 1280).astype(F32)
        squares = squares + jnp.sum((wide * wide).reshape(20, 8, 1280), axis=0)
    squares = jnp.sum(squares, axis=0, keepdims=True)
    scales = jnp.sqrt(jnp.broadcast_to(squares, (128, 1280)) + epsilon)
    s.scale_a[...] = jnp.transpose(scales).reshape(16, 80, 128)
    for made in w_in:
        made.wait_recv()
    for h in range(2):
        at = pl.ds(h * 640, 640)
        total = jnp.zeros((160, 640), F32)
        for n in range(NG):
            right = s.pa[n, :, :, at].reshape(160, 640)
            total = total + jnp.dot(s.w_full[n], right, preferred_element_type=F32)
        s.rot[h] = jnp.transpose(total).astype(BF16)
    swap_r = wires.copy(s.rot.at[1 - c], s.rot_twin, *twin)

    def eigen_base(r, h):
        return s.eig[(z + r) % NZ, :, COLS[h][0] : COLS[h][0] + COLS[h][1]]

    ring_e = Ring(wires, s.e_sent, s.e_got, columns_from_zero, eigen_base, ways)
    n_in = {}

    def eigen(h):
        cols = slice(COLS[h][0], COLS[h][0] + COLS[h][1])
        projected(1, h)
        at = pl.ds(*COLS[h])
        swap_p = wires.copy(s.p.at[:, at], s.p_twin.at[:, at], *twin)
        if h == 0:
            swap_r.wait_recv()
        swap_p.wait_recv()
        total = jnp.dot(s.rot[c], s.p[:, cols], preferred_element_type=F32)
        total = total + jnp.dot(s.rot_twin[...], s.p_twin[:, cols], preferred_element_type=F32)
        s.eig[:, :, cols] = total.reshape(8, 80, COLS[h][1])
        for hop in STARTS:
            if hop[1] == h:
                ring_e.hop(*hop)
        own = s.p[:, cols].astype(F32)
        twins = s.p_twin[:, cols].astype(F32)
        sums = jnp.sum(own * own, axis=0, keepdims=True) + jnp.sum(twins * twins, axis=0, keepdims=True)
        s.norm[:, cols] = jnp.broadcast_to(sums, (8, COLS[h][1]))
        for r in range(1, NZ):
            n_in[r, h] = wires.copy(s.norm.at[:, at], s.norm_got.at[r - 1, :, at], *along_z[r])

    n_far = {}

    def norms(h):
        cols = slice(COLS[h][0], COLS[h][0] + COLS[h][1])
        total = s.norm[:, cols]
        for r in range(1, NZ):
            n_in[r, h].wait_recv()
            total = total + s.norm_got[r - 1, :, cols]
        s.norm_mine[:, cols] = total
        at = pl.ds(*COLS[h])
        n_far[h] = wires.copy(s.norm_mine.at[:, at], s.norm_other.at[:, at], *far)

    e_far = {}

    def eigen_end(h):
        s.e_mine[:, COLS[h][0] : COLS[h][0] + COLS[h][1]] = ring_e.end(h).astype(BF16)
        at = pl.ds(*COLS[h])
        e_far[h] = wires.copy(s.e_mine.at[:, at], s.e_other.at[:, at], *far)

    moves = {}
    to_twin = {0: [], 1: []}

    def pass_on(way, h, d):
        sign = 1 if way == 0 else -1
        view = s.scaled.at[c, (z - sign * d + NZ) % NZ, :, pl.ds(*COLS[h])]
        if d > 0:
            moves[way, h, d].wait_recv()
        if d < (4 if way == h else 3):
            moves[way, h, d + 1] = wires.copy(view, view, *ways[way])
        if d > 0 or way == 0:
            to_twin[h].append(wires.copy(view, view, *twin))

    def scale(h):
        cols = slice(COLS[h][0], COLS[h][0] + COLS[h][1])
        n_far[h].wait_recv()
        scale_g = jnp.sqrt(s.norm_mine[:, cols] + s.norm_other[:, cols] + epsilon)[0:1, :]
        both = s.scale_a[c * 8 + z][:, 0:1] * scale_g
        e_far[h].wait_recv()
        values = (s.e_mine[:, cols].astype(F32) + s.e_other[:, cols].astype(F32)) * (1.0 / math.sqrt(8192.0))
        s.scaled[c, z, :, cols] = (values / both / (both + damping) / both).astype(BF16)
        pass_on(h, h, 0)
        pass_on(1 - h, h, 0)

    eigen(0)
    eigen(1)
    for hop in ((0, 0, 3), (1, 0, 2), (1, 1, 3), (0, 1, 2), (0, 0, 2), (1, 0, 1)):
        ring_e.hop(*hop)
    norms(0)
    for hop in ((1, 1, 2), (0, 1, 1), (0, 0, 1)):
        ring_e.hop(*hop)
    norms(1)
    ring_e.hop(1, 1, 1)
    eigen_end(0)
    eigen_end(1)
    scale(0)
    scale(1)
    for d in range(1, 5):
        for way, h in ((0, 0), (1, 0), (1, 1), (0, 1)):
            if d <= (4 if way == h else 3):
                pass_on(way, h, d)

    rotated = jnp.zeros((1280, 160), F32)
    for h in range(2):
        cols = slice(COLS[h][0], COLS[h][0] + COLS[h][1])
        for made in to_twin[h]:
            made.wait_recv()
        rotated = rotated + lax.dot_general(
            s.scaled[:, :, :, cols].reshape(1280, COLS[h][1]),
            s.p[:, cols],
            (((1,), (1,)), ((), ())),
            preferred_element_type=F32,
        )
    rotated = rotated.astype(BF16)
    o_in = []
    for r in range(1, NG + 1):
        to = (grp + r) % NG
        left = s.pa[to].reshape(160, 1280)
        s.o_sent[r - 1] = jnp.dot(left, rotated, preferred_element_type=F32).astype(BF16)
        if r < NG:
            o_in.append(wires.copy(s.o_sent.at[r - 1], s.o_got.at[r - 1], me, to))
    total = s.o_sent[NG - 1].astype(F32)
    for r in range(1, NG):
        o_in[r - 1].wait_recv()
        total = total + s.o_got[r - 1].astype(F32)
    out[...] = total.astype(BF16)
    wires.drain()


def per_device(activations, out_grads, basis_a, basis_g):
    vmem = pl.BlockSpec(memory_space=pltpu.VMEM)
    hbm = pl.BlockSpec(memory_space=pl.ANY)
    return pl.pallas_call(
        kernel,
        name="refresh",
        out_shape=jax.ShapeDtypeStruct((160, 160), BF16),
        in_specs=[hbm, hbm, vmem, hbm],
        out_specs=vmem,
        scratch_shapes=[pltpu.VMEM(shape, dtype) for shape, dtype in SCRATCH.values()]
        + [
            pltpu.SemaphoreType.DMA((3,)),
            pltpu.SemaphoreType.DMA((COPIES,)),
            pltpu.SemaphoreType.DMA((COPIES,)),
        ],
        compiler_params=pltpu.CompilerParams(
            collective_id=0, has_side_effects=True, vmem_limit_bytes=60 * 2**20
        ),
        cost_estimate=pl.CostEstimate(flops=4 * 10**9, bytes_accessed=10**7, transcendentals=0),
    )(activations, out_grads, basis_a.reshape(2, 80, 1280), basis_g)


def solution(mesh):
    in_specs = (P("dp", None), P("dp", None), P("grp", None), P("grp", None))
    out_specs = P("grp", "dp")
    return jax.shard_map(per_device, mesh=mesh, in_specs=in_specs, out_specs=out_specs, check_vma=False)
```

```python
import math
import types

import jax
import jax.numpy as jnp
from jax import lax
from jax.experimental import pallas as pl
from jax.experimental.pallas import tpu as pltpu
from jax.sharding import PartitionSpec as P

epsilon = 1e-06
damping = 0.1

BF16 = jnp.bfloat16
F32 = jnp.float32
NZ = 8
NX = 4
NG = 8
SENDS = 43
RECVS = 136
ROWS = ((0, 48), (48, 32))
COLS = ((0, 384), (384, 256))
PARTS = ((0, 80), (80, 48), (128, 32))
STARTS = ((0, 0, 4), (1, 1, 4), (0, 1, 3), (1, 0, 3))


def member(z, yh, c):
    return z * 4 + yh * 2 + c


class Wires:
    def __init__(self, send, recv):
        self.send, self.recv, self.sends, self.recvs, self.open = send, recv, 0, 0, []

    def shared_send(self, ref):
        self.sends += 1
        sem = self.send.at[self.sends - 1]
        self.open.append(pltpu.make_async_copy(ref, ref, sem))
        return sem

    def shared_recv(self):
        self.recvs += 1
        return self.recv.at[self.recvs - 1]

    def copy(self, src, dst, to, send=None, recv=None):
        if send is None:
            send = self.shared_send(src)
        if recv is None:
            recv = self.shared_recv()
        made = pltpu.make_async_remote_copy(
            src_ref=src,
            dst_ref=dst,
            send_sem=send,
            recv_sem=recv,
            device_id=to,
            device_id_type=pl.DeviceIdType.MESH,
        )
        made.start()
        return made

    def drain(self):
        for made in self.open:
            made.wait()


def all_of(ref, sem):
    pltpu.make_async_copy(ref, ref, sem).wait()


def down_rows(left, right):
    return lax.dot_general(left, right, (((0,), (0,)), ((), ())), preferred_element_type=F32)


def pack(tile):
    tail = tile[0:40, 128:]
    for n in range(1, 4):
        tail = tail + pltpu.roll(tile[n * 40 : n * 40 + 40, 128:], n * 32, 1)
    return jnp.concatenate([tile[:, :128], tail, jnp.zeros((8, 128), F32)], axis=0)


def unpack(packed):
    tail = packed[160:200]
    lane = lax.broadcasted_iota(jnp.int32, (40, 128), 1)
    pieces = [tail] + [pltpu.roll(tail, 128 - n * 32, 1) for n in range(1, 4)]
    pieces = [jnp.where(lane < 32, piece, 0.0) for piece in pieces]
    return jnp.concatenate([packed[:160], jnp.concatenate(pieces, axis=0)], axis=1)


class Ring:
    def __init__(self, wires, sent, got, base, ways):
        self.wires, self.sent, self.got, self.base, self.ways = wires, sent, got, base, ways
        self.sems = [wires.shared_send(ref) for ref in sent]
        self.links = {}

    def arrived(self, way, h, d):
        self.links[way, h, d].wait_recv()
        return self.got[h][d if way == h else 4 + d].astype(F32)

    def hop(self, way, h, d):
        total = self.base((d if way == 0 else -d) % NZ, h)
        if (way, h, d) in self.links:
            total = total + self.arrived(way, h, d)
        slot = d - 1 if way == h else 3 + d
        self.sent[h][slot] = total.astype(BF16)
        self.links[way, h, d - 1] = self.wires.copy(
            self.sent[h].at[slot], self.got[h].at[slot], self.ways[way], self.sems[h]
        )

    def hops(self, *names):
        for name in names:
            self.hop(*name)

    def step(self, d, h=None):
        self.hops((0, 0, d), (1, 1, d))

    def short(self, d):
        self.hops((0, 1, d), (1, 0, d))

    def end(self, h):
        return self.base(0, h) + self.arrived(0, h, 0) + self.arrived(1, h, 0)


SCRATCH = dict(
    tokens_a=((256, 1280), BF16),
    tokens_g=((256, 5120), BF16),
    basis=((640, 5120), BF16),
    own_a=((256, 256), BF16),
    part_a=((2, 8, 80, 160), BF16),
    pair_a=((8, 80, 160), BF16),
    a_sent0=((7, 48, 160), BF16),
    a_sent1=((7, 32, 160), BF16),
    a_got0=((7, 48, 160), BF16),
    a_got1=((7, 32, 160), BF16),
    a_mine=((80, 160), BF16),
    a_other=((80, 160), BF16),
    a_full=((2, 8, 80, 160), BF16),
    b_full=((8, 2, 80, 1280), BF16),
    pa=((8, 2, 80, 1280), BF16),
    part_f=((8, 2, 2, 160, 640), BF16),
    part_w=((8, 2, 2, 208, 128), BF16),
    pair_f=((8, 2, 160, 640), BF16),
    pair_w=((8, 2, 208, 128), BF16),
    f_sent0=((7, 80, 640), BF16),
    f_sent1=((7, 80, 640), BF16),
    f_got0=((7, 80, 640), BF16),
    f_got1=((7, 80, 640), BF16),
    f_final=((2, 80, 640), BF16),
    f_other=((80, 640), BF16),
    early_sent=((8, 80, 640), BF16),
    early_got=((8, 80, 640), BF16),
    l_sent0=((7, 48, 640), BF16),
    l_sent1=((7, 32, 640), BF16),
    l_got0=((7, 48, 640), BF16),
    l_got1=((7, 32, 640), BF16),
    w_sent0=((7, 208, 128), BF16),
    w_sent1=((7, 208, 128), BF16),
    w_got0=((7, 208, 128), BF16),
    w_got1=((7, 208, 128), BF16),
    w_final=((2, 208, 128), BF16),
    w_other=((208, 128), BF16),
    w_full=((8, 208, 128), BF16),
    f=((160, 640), BF16),
    p_sent=((8, 160, 640), BF16),
    p_got=((7, 160, 640), BF16),
    p=((160, 640), BF16),
    p_twin=((160, 640), BF16),
    rot=((2, 640, 160), BF16),
    rot_twin=((640, 160), BF16),
    scale_a=((16, 80, 128), F32),
    eig=((8, 80, 640), F32),
    norm=((8, 640), F32),
    norm_got=((7, 8, 640), F32),
    norm_mine=((8, 640), F32),
    norm_other=((8, 640), F32),
    e_sent0=((7, 80, 384), BF16),
    e_sent1=((7, 80, 256), BF16),
    e_got0=((7, 80, 384), BF16),
    e_got1=((7, 80, 256), BF16),
    e_mine=((80, 640), BF16),
    e_other=((80, 640), BF16),
    scaled=((2, 8, 80, 640), BF16),
    o_sent=((8, 208, 128), BF16),
    o_got=((7, 208, 128), BF16),
)


def kernel(act, grads, b_own, b_g, out, *scratch):
    s = types.SimpleNamespace(**dict(zip(SCRATCH, scratch)))
    load, send, recv = scratch[len(SCRATCH) :]
    dp = lax.axis_index("dp")
    grp = lax.axis_index("grp")
    z, yh, c = dp // 4, (dp // 2) % 2, dp % 2
    yl, x = grp // NX, grp % NX
    me = dp
    others = [(me, (grp + r) % NG) for r in range(NG)]
    twin = (member(z, yh, 1 - c), grp)
    far = (member(z, 1 - yh, c), grp)
    cross = (1 - yl) * NX + x
    up = (member(z, (yh + yl) % 2, c), cross)
    down = (member(z, (yh + 1 - yl) % 2, c), cross)
    along_z = [(member((z + r) % NZ, yh, c), grp) for r in range(NZ)]
    along_x = [(me, yl * NX + (x + r) % NX) for r in range(NX)]
    ways = (along_z[1], along_z[NZ - 1])
    wires = Wires(send, recv)

    loads = [
        pltpu.make_async_copy(act, s.tokens_a, load.at[0]),
        pltpu.make_async_copy(grads, s.tokens_g, load.at[1]),
        pltpu.make_async_copy(b_g, s.basis, load.at[2]),
    ]
    for made in loads:
        made.start()
    peers = [twin, far, (member(z, 1 - yh, c), cross)] + along_z[1:] + others[1:]
    barrier = pltpu.get_barrier_semaphore()
    for peer in peers:
        pl.semaphore_signal(barrier, inc=1, device_id=peer, device_id_type=pl.DeviceIdType.MESH)

    loads[0].wait()
    first = lax.broadcasted_iota(jnp.int32, (1280, 256), 0)
    second = lax.broadcasted_iota(jnp.int32, (1280, 256), 1)
    chosen = jnp.where((first == second + grp * 160) & (second < 160), 1.0, 0.0).astype(BF16)
    s.own_a[...] = jnp.dot(s.tokens_a[...], chosen, preferred_element_type=F32).astype(BF16)
    for half in range(2):
        share = down_rows(s.tokens_a[:, half * 640 : half * 640 + 640], s.own_a[:, 0:160])
        s.part_a[half] = share.astype(BF16).reshape(8, 80, 160)

    loads[1].wait()
    own_columns = pl.ds(pl.multiple_of(grp * 640, 128), 640)
    swaps_f, ready_f = {}, set()
    swap_f_send = wires.shared_send(s.pair_f)
    swap_w_send = wires.shared_send(s.pair_w)
    swap_w_recv = wires.shared_recv()

    def block(r):
        zz = (z + r) % NZ
        left = s.tokens_g[:, pl.ds(pl.multiple_of(zz * 640, 128), 640)]
        for_f = down_rows(left, s.tokens_g[:, own_columns])
        for_w = down_rows(left, s.own_a[...])
        for h in range(2):
            for cc in range(2):
                rows = slice((h * 2 + cc) * 160, (h * 2 + cc) * 160 + 160)
                s.part_f[zz, cc, h] = for_f[rows].astype(BF16)
                s.part_w[zz, cc, h] = pack(for_w[rows]).astype(BF16)

    def swap(r):
        zz = (z + r) % NZ
        swaps_f[r] = wires.copy(s.part_f.at[zz, 1 - c], s.pair_f.at[r], twin, swap_f_send)
        wires.copy(s.part_w.at[zz, 1 - c], s.pair_w.at[r], twin, swap_w_send, swap_w_recv)

    def share_f(r, h, rows):
        if r not in ready_f:
            ready_f.add(r)
            swaps_f[r].wait_recv()
        zz = (z + r) % NZ
        return s.part_f[zz, c, h, rows, :].astype(F32) + s.pair_f[r, h, rows, :].astype(F32)

    def share_w(r, h):
        return s.part_w[(z + r) % NZ, c, h].astype(F32) + s.pair_w[r, h].astype(F32)

    def share_a(r, h):
        zz = (z + r) % NZ
        rows = slice(ROWS[h][0], ROWS[h][0] + ROWS[h][1])
        return s.part_a[c, zz, rows].astype(F32) + s.pair_a[zz, rows].astype(F32)

    early, early_ready = {}, set()
    early_send = wires.shared_send(s.early_sent)

    def send_early(r):
        s.early_sent[r] = share_f(r, 1 - yh, slice(80, 160)).astype(BF16)
        early[r] = wires.copy(s.early_sent.at[r], s.early_got.at[r], far, early_send)

    def late(r, h):
        if r not in early_ready:
            early_ready.add(r)
            early[r].wait_recv()
        start, count = ROWS[h]
        rows = slice(start, start + count)
        return share_f(r, yh, slice(80 + start, 80 + start + count)) + s.early_got[r, rows].astype(F32)

    ring_f = Ring(wires, (s.f_sent0, s.f_sent1), (s.f_got0, s.f_got1), lambda r, h: share_f(r, h, slice(0, 80)), ways)
    ring_w = Ring(wires, (s.w_sent0, s.w_sent1), (s.w_got0, s.w_got1), share_w, ways)
    ring_a = Ring(wires, (s.a_sent0, s.a_sent1), (s.a_got0, s.a_got1), share_a, ways)
    ring_l = Ring(wires, (s.l_sent0, s.l_sent1), (s.l_got0, s.l_got1), late, ways)

    block(4)
    block(3)
    pl.semaphore_wait(barrier, len(peers))
    swap_a = wires.copy(s.part_a.at[1 - c], s.pair_a, twin)
    swap(4)
    swap(3)

    b_y_send, b_y_recv = wires.shared_send(b_own.at[c]), wires.shared_recv()
    for part, to in enumerate((up, down)):
        rows = pl.ds(*ROWS[part])
        wires.copy(b_own.at[c, rows], s.b_full.at[grp, c, rows], to, b_y_send, b_y_recv)
    b_x_send = wires.shared_send(s.b_full.at[pl.ds(0, 6), 0])
    b_x_recv, b_x2_recv = wires.shared_recv(), wires.shared_recv()
    for r in range(1, NX):
        wires.copy(b_own.at[c], s.b_full.at[grp, c], along_x[r], b_x_send, b_x_recv)
    b_twin_send, b_twin_recv = wires.shared_send(s.b_full.at[pl.ds(0, 7), 0]), wires.shared_recv()
    s.b_full[grp] = b_own[...]

    def b_across():
        view = s.b_full.at[cross, c]
        all_of(view, b_y_recv)
        for r in range(1, NX):
            wires.copy(view, view, along_x[r], b_x_send, b_x2_recv)
        wires.copy(view, view, twin, b_twin_send, b_twin_recv)

    def b_along():
        for row, sem in ((yl, b_x_recv), (1 - yl, b_x2_recv)):
            all_of(s.b_full.at[pl.ds(0, 3), 0], sem)
            for r in range(1, NX):
                view = s.b_full.at[row * NX + (x + NX - r) % NX, c]
                wires.copy(view, view, twin, b_twin_send, b_twin_recv)

    block(5)
    swap(5)
    swap_a.wait_recv()
    ring_a.hops(*STARTS)
    ring_f.hops(*STARTS)
    block(2)
    swap(2)
    send_early(4)
    send_early(3)
    send_early(5)
    block(6)
    swap(6)
    b_across()
    ring_a.step(3)
    ring_f.step(3)
    send_early(2)
    block(1)
    swap(1)
    send_early(6)
    ring_a.short(2)
    ring_f.short(2)
    block(7)
    swap(7)
    send_early(1)
    ring_a.step(2)
    ring_f.step(2)
    block(0)
    swap(0)
    send_early(7)
    ring_a.short(1)
    ring_f.short(1)
    send_early(0)
    ring_a.step(1)
    ring_f.step(1)
    all_of(s.pair_w, swap_w_recv)
    ring_w.hops(*STARTS)

    for h in range(2):
        s.a_mine[ROWS[h][0] : ROWS[h][0] + ROWS[h][1], :] = ring_a.end(h).astype(BF16)
    a_far = wires.copy(s.a_mine, s.a_other, far)
    for h in range(2):
        s.f_final[h] = ring_f.end(h).astype(BF16)
    f_far = wires.copy(s.f_final.at[1 - yh], s.f_other, far)
    ring_l.hops(*STARTS)
    ring_w.step(3)
    a_far.wait_recv()
    s.a_full[c, z] = ((s.a_mine[...].astype(F32) + s.a_other[...].astype(F32)) / 8192.0).astype(BF16)
    a_rows_send, a_rows_recv = wires.shared_send(s.a_full.at[0, pl.ds(0, 7)]), wires.shared_recv()
    for r in range(1, NZ):
        wires.copy(s.a_full.at[c, z], s.a_full.at[c, z], along_z[r], a_rows_send, a_rows_recv)
    ring_l.step(3)
    ring_w.short(2)

    p_recv = {}

    def project(n):
        start, count = PARTS[n]
        rows = pl.ds(start, count)
        cuts = COLS if n == 2 else ((0, 640),)
        send = wires.shared_send(s.p_sent.at[pl.ds(0, 7), rows])
        for h in range(len(cuts)):
            p_recv[n, h] = wires.shared_recv()
        for r in range(1, NG + 1):
            to = (grp + r) % NG
            at = pl.ds(pl.multiple_of(to * 640, 128), 640)
            chunk = jnp.dot(s.f[rows, :], s.basis[:, at], preferred_element_type=F32)
            s.p_sent[r - 1, rows, :] = chunk.astype(BF16)
            if r < NG:
                for h, cut in enumerate(cuts):
                    view = (r - 1, rows, pl.ds(*cut))
                    wires.copy(s.p_sent.at[view], s.p_got.at[view], others[r], send, p_recv[n, h])

    def projected(n, h):
        rows, cols = pl.ds(*PARTS[n]), pl.ds(*(COLS[h] if n == 2 else (0, 640)))
        all_of(s.p_got.at[:, rows, cols], p_recv[n, h])
        total = s.p_sent[NG - 1, rows, cols].astype(F32)
        for r in range(1, NG):
            total = total + s.p_got[r - 1, rows, cols].astype(F32)
        s.p[rows, cols] = total.astype(BF16)

    f_far.wait_recv()
    s.f[0:80, :] = ((s.f_final[yh].astype(F32) + s.f_other[...].astype(F32)) / 8192.0).astype(BF16)
    loads[2].wait()
    project(0)

    ring_l.short(2)
    ring_w.step(2)
    ring_l.step(2)
    all_of(s.a_full.at[0, pl.ds(0, 7)], a_rows_recv)
    a_half = wires.copy(s.a_full.at[c], s.a_full.at[c], twin)
    b_along()
    ring_w.short(1)
    ring_l.short(1)

    a_half.wait_recv()
    all_of(s.b_full.at[pl.ds(0, 7), 0], b_twin_recv)
    left = s.a_full[...].reshape(1280, 160)
    for n in range(5):
        at = pl.ds(n * 256, 256)
        product = down_rows(left, s.b_full[:, :, :, at].reshape(1280, 256))
        s.pa[grp, :, :, at] = product.astype(BF16).reshape(2, 80, 256)
    pa_y_send = wires.shared_send(s.pa.at[pl.ds(0, 4), 0])
    pa_y_recv = [wires.shared_recv() for r in range(NX)]
    pa_twin_send, pa_twin_recv = wires.shared_send(s.pa.at[pl.ds(0, 7), 0]), wires.shared_recv()
    pa_x_send = wires.shared_send(s.pa.at[pl.ds(0, 3), 0])

    def pa_across(r):
        owner = yl * NX + (x + NX - r) % NX
        for part, to in enumerate((up, down)):
            view = s.pa.at[owner, c, pl.ds(*ROWS[part])]
            wires.copy(view, view, to, pa_y_send, pa_y_recv[r])

    pa_x = [wires.copy(s.pa.at[grp, c], s.pa.at[grp, c], along_x[r], pa_x_send) for r in range(1, NX)]
    pa_across(0)

    ring_w.step(1)
    ring_l.step(1)
    for h in range(2):
        s.w_final[h] = ring_w.end(h).astype(BF16)
    w_far = wires.copy(s.w_final.at[1 - yh], s.w_other, far)
    for h in range(2):
        s.f[80 + ROWS[h][0] : 80 + ROWS[h][0] + ROWS[h][1], :] = (ring_l.end(h) / 8192.0).astype(BF16)
        project(1 + h)
    w_far.wait_recv()
    s.w_full[grp] = (s.w_final[yh].astype(F32) + s.w_other[...].astype(F32)).astype(BF16)
    w_send, w_recv = wires.shared_send(s.w_full.at[pl.ds(0, 7)]), wires.shared_recv()
    for r in range(1, NG):
        wires.copy(s.w_full.at[grp], s.w_full.at[grp], others[r], w_send, w_recv)
    for r in range(1, NX):
        pa_x[r - 1].wait_recv()
        pa_across(r)
        view = s.pa.at[yl * NX + (x + NX - r) % NX, c]
        wires.copy(view, view, twin, pa_twin_send, pa_twin_recv)
    projected(0, 0)
    for r in range(NX):
        view = s.pa.at[(1 - yl) * NX + (x + NX - r) % NX, c]
        all_of(view, pa_y_recv[r])
        wires.copy(view, view, twin, pa_twin_send, pa_twin_recv)

    all_of(s.pa.at[pl.ds(0, 7), 0], pa_twin_recv)
    squares = jnp.zeros((8, 1280), F32)
    for n in range(NG):
        wide = s.pa[n].reshape(160, 1280).astype(F32)
        squares = squares + jnp.sum((wide * wide).reshape(20, 8, 1280), axis=0)
    squares = jnp.sum(squares, axis=0, keepdims=True)
    scales = jnp.sqrt(jnp.broadcast_to(squares, (128, 1280)) + epsilon)
    s.scale_a[...] = jnp.transpose(scales).reshape(16, 80, 128)
    projected(1, 0)
    all_of(s.w_full.at[pl.ds(0, 7)], w_recv)
    for h in range(2):
        at = pl.ds(h * 640, 640)
        total = jnp.zeros((160, 640), F32)
        for n in range(NG):
            weight = unpack(s.w_full[n].astype(F32))[:, 0:160].astype(BF16)
            right = s.pa[n, :, :, at].reshape(160, 640)
            total = total + jnp.dot(weight, right, preferred_element_type=F32)
        s.rot[h] = jnp.transpose(total).astype(BF16)
    swap_r = wires.copy(s.rot.at[1 - c], s.rot_twin, twin)

    def eigen_base(r, h):
        return s.eig[(z + r) % NZ, :, COLS[h][0] : COLS[h][0] + COLS[h][1]]

    ring_e = Ring(wires, (s.e_sent0, s.e_sent1), (s.e_got0, s.e_got1), eigen_base, ways)
    n_recv, n_far, e_far = {}, {}, {}

    def eigen(h):
        cols = pl.ds(*COLS[h])
        projected(2, h)
        swap_p = wires.copy(s.p.at[:, cols], s.p_twin.at[:, cols], twin)
        if h == 0:
            swap_r.wait_recv()
        swap_p.wait_recv()
        total = jnp.dot(s.rot[c], s.p[:, cols], preferred_element_type=F32)
        total = total + jnp.dot(s.rot_twin[...], s.p_twin[:, cols], preferred_element_type=F32)
        s.eig[:, :, cols] = total.reshape(8, 80, COLS[h][1])
        ring_e.hops(*[name for name in STARTS if name[1] == h])
        own = s.p[:, cols].astype(F32)
        twins = s.p_twin[:, cols].astype(F32)
        sums = jnp.sum(own * own, axis=0, keepdims=True) + jnp.sum(twins * twins, axis=0, keepdims=True)
        s.norm[:, cols] = jnp.broadcast_to(sums, (8, COLS[h][1]))
        n_send = wires.shared_send(s.norm_got.at[:, :, cols])
        n_recv[h] = wires.shared_recv()
        for r in range(1, NZ):
            wires.copy(s.norm.at[:, cols], s.norm_got.at[r - 1, :, cols], along_z[r], n_send, n_recv[h])

    def norms(h):
        cols = pl.ds(*COLS[h])
        all_of(s.norm_got.at[:, :, cols], n_recv[h])
        total = s.norm[:, cols]
        for r in range(1, NZ):
            total = total + s.norm_got[r - 1, :, cols]
        s.norm_mine[:, cols] = total
        n_far[h] = wires.copy(s.norm_mine.at[:, cols], s.norm_other.at[:, cols], far)

    def eigen_end(h):
        cols = pl.ds(*COLS[h])
        s.e_mine[:, cols] = ring_e.end(h).astype(BF16)
        e_far[h] = wires.copy(s.e_mine.at[:, cols], s.e_other.at[:, cols], far)

    moves = {}
    move_send = [wires.shared_send(s.scaled.at[0, pl.ds(0, 7), :, pl.ds(*COLS[h])]) for h in range(2)]
    twin_send = [wires.shared_send(s.scaled.at[0, :, :, pl.ds(*COLS[h])]) for h in range(2)]
    twin_recv = [wires.shared_recv() for h in range(2)]

    def pass_on(way, h, d):
        sign = 1 if way == 0 else -1
        view = s.scaled.at[c, (z - sign * d + NZ) % NZ, :, pl.ds(*COLS[h])]
        if d > 0:
            moves[way, h, d].wait_recv()
        if d < (4 if way == h else 3):
            moves[way, h, d + 1] = wires.copy(view, view, ways[way], move_send[h])
        if d > 0 or way == 0:
            wires.copy(view, view, twin, twin_send[h], twin_recv[h])

    def scale(h):
        cols = pl.ds(*COLS[h])
        n_far[h].wait_recv()
        scale_g = jnp.sqrt(s.norm_mine[:, cols] + s.norm_other[:, cols] + epsilon)[0:1, :]
        both = s.scale_a[c * 8 + z][:, 0:1] * scale_g
        e_far[h].wait_recv()
        values = (s.e_mine[:, cols].astype(F32) + s.e_other[:, cols].astype(F32)) * (1.0 / math.sqrt(8192.0))
        s.scaled[c, z, :, cols] = (values / both / (both + damping) / both).astype(BF16)
        pass_on(h, h, 0)
        pass_on(1 - h, h, 0)

    eigen(0)
    eigen(1)
    ring_e.hops((0, 0, 3), (1, 0, 2), (1, 1, 3), (0, 1, 2), (0, 0, 2), (1, 0, 1))
    norms(0)
    ring_e.hops((1, 1, 2), (0, 1, 1), (0, 0, 1))
    norms(1)
    ring_e.hop(1, 1, 1)
    eigen_end(0)
    eigen_end(1)
    scale(0)
    scale(1)
    for d in range(1, 5):
        for way, h in ((0, 0), (1, 0), (1, 1), (0, 1)):
            if d <= (4 if way == h else 3):
                pass_on(way, h, d)

    rotated = jnp.zeros((1280, 160), F32)
    for h in range(2):
        cols = pl.ds(*COLS[h])
        all_of(s.scaled.at[0, :, :, cols], twin_recv[h])
        rotated = rotated + lax.dot_general(
            s.scaled[:, :, :, cols].reshape(1280, COLS[h][1]),
            s.p[:, cols],
            (((1,), (1,)), ((), ())),
            preferred_element_type=F32,
        )
    rotated = jnp.concatenate([rotated, jnp.zeros((1280, 96), F32)], axis=1).astype(BF16)
    o_send, o_recv = wires.shared_send(s.o_got), wires.shared_recv()
    for r in range(1, NG + 1):
        left = s.pa[(grp + r) % NG].reshape(160, 1280)
        s.o_sent[r - 1] = pack(jnp.dot(left, rotated, preferred_element_type=F32)).astype(BF16)
        if r < NG:
            wires.copy(s.o_sent.at[r - 1], s.o_got.at[r - 1], others[r], o_send, o_recv)
    all_of(s.o_got, o_recv)
    total = s.o_sent[NG - 1].astype(F32)
    for r in range(1, NG):
        total = total + s.o_got[r - 1].astype(F32)
    out[...] = unpack(total)[:, 0:160].astype(BF16)
    wires.drain()


def per_device(activations, out_grads, basis_a, basis_g):
    vmem = pl.BlockSpec(memory_space=pltpu.VMEM)
    hbm = pl.BlockSpec(memory_space=pl.ANY)
    return pl.pallas_call(
        kernel,
        name="refresh",
        out_shape=jax.ShapeDtypeStruct((160, 160), BF16),
        in_specs=[hbm, hbm, vmem, hbm],
        out_specs=vmem,
        scratch_shapes=[pltpu.VMEM(shape, dtype) for shape, dtype in SCRATCH.values()]
        + [
            pltpu.SemaphoreType.DMA((3,)),
            pltpu.SemaphoreType.DMA((SENDS,)),
            pltpu.SemaphoreType.DMA((RECVS,)),
        ],
        compiler_params=pltpu.CompilerParams(
            collective_id=0, has_side_effects=True, vmem_limit_bytes=60 * 2**20
        ),
        cost_estimate=pl.CostEstimate(flops=4 * 10**9, bytes_accessed=10**7, transcendentals=0),
    )(activations, out_grads, basis_a.reshape(2, 80, 1280), basis_g)


def solution(mesh):
    in_specs = (P("dp", None), P("dp", None), P("grp", None), P("grp", None))
    out_specs = P("grp", "dp")
    return jax.shard_map(per_device, mesh=mesh, in_specs=in_specs, out_specs=out_specs, check_vma=False)
```
